256 devices in a mesh: segment: 4 (over x), expert: 64 (over z, y, core).
Axes of the slice: x: 4, y: 4, z: 8, core: 2. Of those that a mesh axis runs over, the one named last changes fastest.
Arguments:
- tokens: bfloat16 [2, 4096, 3584], P(None, 'expert'), may hold values from -6 to 6
- norm_gain: float32 [4, 2, 3584], P('segment'), may hold values from 0.1 to 1.9
- gate_weight: bfloat16 [4, 2, 3584, 16384], P('segment', None, None, 'expert'), may hold values from -0.09375 to 0.09375
- up_weight: bfloat16 [4, 2, 3584, 16384], P('segment', None, None, 'expert'), may hold values from -0.09375 to 0.09375
- down_weight: bfloat16 [4, 2, 16384, 3584], P('segment', None, 'expert'), may hold values from -0.125 to 0.125
- expert_ids: int32 [4, 2, 2, 4096], P('segment', None, None, 'expert'), may hold values from 0 to 8, as said below
- gate_scale: float32 [4, 2, 2, 4096], P('segment', None, None, 'expert'), may hold values from 0.5 to 2
- depths: int32 [4], P('segment'), may hold values from 1 to 2, as said below
Outputs:
- section_out: bfloat16 [4, 2, 4096, 3584], P('segment', None, 'expert')
The draws below stay inside these ranges and needn't reach their ends.
Inputs may be any that keep to these rules, and one draw needn't show every extreme that they name: `expert_ids`: 8 marks a token routed outside this layer's experts. In each aligned block of 64 tokens (one device's tokens of one section, layer and micro-batch) exactly 8 tokens name an expert below 8; no expert is named by more than 2 of them, and one by exactly 2. `depths`: at least one section applies 2 layers and at least one applies 1.
All inputs are finite; a program needn't handle non-finite values.
Results may differ from the reference program's by a relative error of at most 0.012.
Values may be sent and summed in bfloat16 or wider, within the bound.
A program may use at most 128 MiB of HBM per device.

```python
import jax
import jax.numpy as jnp
from jax import lax

D = 3584
FF_E = 2048
GROUP = 8
HID_DEV = 256
EXP_WIN = 8
LMAX = 2
MB = 2
TOK_DEV = 64
TOKENS = 4096
ROUTED = 8
CAP = 2
SECTIONS = 4


def block_routes(key):
    key_lead, key_pick, key_place = jax.random.split(key, 3)
    leading = jax.random.randint(key_lead, (), 0, EXP_WIN).astype(jnp.int32)
    spare = (EXP_WIN - 1) * CAP
    offsets = jnp.arange(spare, dtype=jnp.int32) // CAP
    others = (leading + 1 + offsets) % EXP_WIN
    scores = jax.random.randint(key_pick, (spare,), 0, 1 << 20) * spare + jnp.arange(spare)
    others = others[jnp.argsort(scores)][:ROUTED - CAP]
    labels = jnp.concatenate([jnp.full((CAP,), leading, jnp.int32), others.astype(jnp.int32), jnp.full((TOK_DEV - ROUTED,), EXP_WIN, jnp.int32)])
    placing = jax.random.randint(key_place, (TOK_DEV,), 0, 1 << 20) * TOK_DEV + jnp.arange(TOK_DEV)
    return labels[jnp.argsort(placing)]


def draw_expert_ids(key, part):
    key = jax.random.fold_in(key, 11)
    blocks = SECTIONS * LMAX * MB * (TOKENS // TOK_DEV)
    block_keys = jax.random.split(key, blocks)
    return jax.vmap(block_routes)(block_keys).reshape(SECTIONS, LMAX, MB, TOKENS)


def draw_depths(key, part):
    key = jax.random.fold_in(key, 23)
    key_base, key_order = jax.random.split(key)
    base = jax.random.randint(key_base, (SECTIONS,), 1, LMAX + 1).astype(jnp.int32)
    ordering = jnp.argsort(jax.random.randint(key_order, (SECTIONS,), 0, 1 << 20) * SECTIONS + jnp.arange(SECTIONS))
    base = base.at[ordering[0]].set(LMAX)
    base = base.at[ordering[1]].set(1)
    return base


def block_levels(key, shape, cuts, low, high):
    level = 1.0
    for dim, shards_of in cuts:
        heights = jax.random.uniform(jax.random.fold_in(jax.random.fold_in(key, 6), dim), (shards_of,), jnp.float32, low / len(cuts), high / len(cuts))
        level = level * jnp.repeat(jnp.exp(heights), shape[dim] // shards_of).reshape((-1,) + (1,) * (len(shape) - 1 - dim))
    return level


def centred(key, extent, scale, reach, shards=(), held_as=jnp.bfloat16):
    array = jax.random.normal(key, extent, jnp.float32) * scale
    if len(shards) > 0:
        array = block_levels(key, extent, shards, -0.22, 0.18) * array
    return jnp.clip(array, min=-reach, max=reach).astype(held_as)


def setup_inputs(seed: int = 0) -> dict:
    seeds = jax.random.split(jax.random.key(seed), 9)
    tokens = centred(seeds[0], (MB, TOKENS, D), 1.0, 6.0, ((1, 64),))
    norm_gain = jnp.clip(1.0 + 0.18 * jax.random.normal(seeds[1], (SECTIONS, LMAX, D), jnp.float32), 0.1, 1.9)
    gate_weight = centred(seeds[2], (SECTIONS, LMAX, D, EXP_WIN * FF_E), D ** -0.5, 0.09375, ((0, 4), (3, 64)))
    up_weight = centred(seeds[3], (SECTIONS, LMAX, D, EXP_WIN * FF_E), D ** -0.5, 0.09375, ((0, 4), (3, 64)))
    down_weight = centred(seeds[4], (SECTIONS, LMAX, EXP_WIN * FF_E, D), FF_E ** -0.5, 0.125, ((0, 4), (2, 64)))
    expert_ids = draw_expert_ids(jax.random.fold_in(seeds[8], 71), 0)
    gate_scale = jnp.clip(0.5 + 1.5 * jax.random.uniform(seeds[6], (SECTIONS, LMAX, MB, TOKENS), jnp.float32) ** block_levels(seeds[6], (SECTIONS, LMAX, MB, TOKENS), ((0, 4), (3, 64)), -0.2, 0.2), 0.5, 2.0)
    depths = draw_depths(jax.random.fold_in(seeds[8], 71), 0)
    return dict(tokens=tokens, norm_gain=norm_gain, gate_weight=gate_weight, up_weight=up_weight, down_weight=down_weight, expert_ids=expert_ids, gate_scale=gate_scale, depths=depths)


def norm_rows(state, gain):
    widened = state.astype(jnp.float32)
    ratio = lax.rsqrt(lax.optimization_barrier(jnp.mean(widened * widened, axis=-1, keepdims=True)) + 1e-06)
    return (widened * ratio * gain).astype(jnp.bfloat16)

def expert_layer(state, gain, gate_w, up_w, down_w, routing, scaling):
    normed = norm_rows(state, gain)
    bound = TOKENS // TOK_DEV * CAP
    combined = jnp.zeros((TOKENS, D), jnp.float32)
    for expert in range(EXP_WIN):
        ordering = jnp.argsort((routing != expert).astype(jnp.int32), stable=True)[:bound].astype(jnp.int32)
        matched = routing[ordering] == expert
        gathered = normed[ordering]
        columns = slice(expert * FF_E, (expert + 1) * FF_E)
        gate_pre = jnp.dot(gathered, gate_w[:, columns], preferred_element_type=jnp.float32)
        up_pre = jnp.dot(gathered, up_w[:, columns], preferred_element_type=jnp.float32)
        hidden = (jax.nn.silu(gate_pre) * up_pre).astype(jnp.bfloat16)
        blocks = hidden.reshape(bound, GROUP, HID_DEV).astype(jnp.float32)
        down_blocks = down_w[columns].reshape(GROUP, HID_DEV, D).astype(jnp.float32)
        partials = jnp.einsum('rgk,gkd->rgd', blocks, down_blocks).astype(jnp.bfloat16)
        expert_out = lax.optimization_barrier(jnp.sum(partials.astype(jnp.float32), axis=1))
        expert_out = jnp.where(matched[:, None], expert_out, jnp.zeros_like(expert_out))
        combined = combined.at[ordering].add(expert_out)
    return (state.astype(jnp.float32) + scaling[:, None] * combined).astype(jnp.bfloat16)

def reference(tokens, norm_gain, gate_weight, up_weight, down_weight, expert_ids, gate_scale, depths):
    current = [tokens[batch_idx] for batch_idx in range(MB)]
    outputs = []
    for section in range(SECTIONS):
        section_rows = []
        for batch_idx in range(MB):
            state = current[batch_idx]
            for layer_idx in range(LMAX):

                def apply(value, section=section, layer_idx=layer_idx, batch_idx=batch_idx):
                    return expert_layer(value, norm_gain[section, layer_idx], gate_weight[section, layer_idx], up_weight[section, layer_idx], down_weight[section, layer_idx], expert_ids[section, layer_idx, batch_idx], gate_scale[section, layer_idx, batch_idx])

                def keep(value):
                    return value
                state = lax.cond(layer_idx < depths[section], apply, keep, state)
            current[batch_idx] = state
            section_rows.append(state)
        outputs.append(jnp.stack(section_rows))
    return jnp.stack(outputs)
```

```python
import functools

import jax
import jax.numpy as jnp
from jax import lax
from jax.experimental import pallas as pl
from jax.experimental.pallas import tpu as pltpu
from jax.sharding import PartitionSpec as P

MESH = pl.DeviceIdType.MESH
LMAX = 2
MB = 2
TOK = 64
Z = 8
Y = 4
PIECE = 512
FAR_FIRST = (4, 3, 5, 2, 6, 1, 7, 0)


def iota(shape, dim):
    return lax.broadcasted_iota(jnp.int32, shape, dim)


def ones_where(condition):
    return jnp.where(condition, 1.0, 0.0).astype(jnp.bfloat16)


def dot(a, b):
    return jnp.dot(a, b, preferred_element_type=jnp.float32)


def kernel(
    starts,
    steps,
    tokens_ref,
    gain_ref,
    gate_hbm,
    up_hbm,
    down_hbm,
    ids_ref,
    ids_col_ref,
    scale_ref,
    depth_ref,
    out_ref,
    gate_w,
    up_w,
    down_w,
    state,
    ids_next,
    pack_m,
    unpack_m,
    perm,
    perm_t,
    sent,
    landed,
    gathered,
    part,
    sibling_part,
    pair,
    reduced,
    back,
    returned,
    weight_sem,
    state_sem,
    ids_sem,
    sent_sem,
    landed_sem,
    gather_send_sem,
    gather_sem,
    sib_sem,
    reduce_send_sem,
    reduce_sem,
    back_sem,
    returned_sem,
):
    x = lax.axis_index("segment")
    me = lax.axis_index("expert")
    segments = lax.axis_size("segment")
    z = me // (Y * 2)
    y = (me // 2) % Y
    c = me % 2
    width = tokens_ref.shape[2]
    pieces = width // PIECE
    group = Y * 16

    def at(xx, zz, yy, cc):
        return (xx, zz * (Y * 2) + yy * 2 + cc)

    loads = []
    for layer in range(LMAX):
        for i, (src, dst) in enumerate(((gate_hbm, gate_w), (up_hbm, up_w), (down_hbm, down_w))):
            load = pltpu.make_async_copy(src.at[0, layer], dst.at[layer], weight_sem.at[layer, i])
            load.start()
            loads.append(load)

    barrier = pltpu.get_barrier_semaphore()

    def greet(device):
        pl.semaphore_signal(barrier, inc=1, device_id=device, device_id_type=MESH)

    for d in range(1, Z):
        greet(at(x, (z + d) % Z, y, c))
    for d in range(1, Y):
        greet(at(x, z, (y + d) % Y, c))
    greet(at(x, z, y, 1 - c))

    @pl.when(x > 0)
    def _():
        for d in range(Z):
            greet(at(x - 1, (z + d) % Z, y, c))

    @pl.when(x < segments - 1)
    def _():
        for d in range(Z):
            greet(at(x + 1, (z + d) % Z, y, c))

    @pl.when((x == 0) | (x == segments - 1))
    def _():
        pl.semaphore_wait(barrier, 11 + Z)

    @pl.when((x > 0) & (x < segments - 1))
    def _():
        pl.semaphore_wait(barrier, 11 + 2 * Z)

    ids_copy = pltpu.make_async_remote_copy(
        src_ref=ids_ref,
        dst_ref=ids_next,
        send_sem=ids_sem.at[0],
        recv_sem=ids_sem.at[1],
        device_id=at(jnp.maximum(x - 1, 0), z, y, c),
        device_id_type=MESH,
    )

    @pl.when(x > 0)
    def _():
        ids_copy.start()

    lanes = pieces * TOK
    row = iota((128, lanes), 0)
    col = iota((128, lanes), 1)
    row_e, row_j, row_k = row // 16, (row // 2) % 8, row % 2
    earlier = ones_where(iota((TOK, lanes), 0) <= iota((TOK, lanes), 1) % TOK)
    same_j = row_j == col // TOK

    def packing(ids_row):
        hit = ones_where(jnp.broadcast_to(ids_row, (128, lanes)) == row_e)
        rank = dot(hit[:, :TOK], earlier)
        good = (hit > 0) & (rank == (row_k + 1).astype(jnp.float32)) & same_j
        return ones_where(good)

    slot = iota((TOK, 128), 1)
    slot_e, slot_j, slot_k = slot // 16, (slot // 2) % 8, slot % 2
    earlier_t = ones_where(iota((TOK, TOK), 1) <= iota((TOK, TOK), 0))

    def dispatch_copy(m, zz, to):
        return pltpu.make_async_remote_copy(
            src_ref=sent.at[m, zz],
            dst_ref=landed.at[m, z],
            send_sem=sent_sem.at[m, zz],
            recv_sem=landed_sem.at[m, z],
            device_id=at(to, zz, y, c),
            device_id_type=MESH,
        )

    def own_copy(m):
        return pltpu.make_async_copy(sent.at[m, z], landed.at[m, z], landed_sem.at[m, z])

    def dispatch(which, m, to):
        sent[m] = (
            dot(pack_m[which, m], state[m])
            .astype(jnp.bfloat16)
            .reshape(Z, 16, PIECE)
        )
        for d in FAR_FIRST[:-1]:
            dispatch_copy(m, (z + d) % Z, to).start()

        @pl.when(to == x)
        def _():
            own_copy(m).start()

        @pl.when(to != x)
        def _():
            dispatch_copy(m, z, to).start()

    def dispatch_sent(m, to):
        for d in FAR_FIRST[:-1]:
            dispatch_copy(m, (z + d) % Z, to).wait_send()

        @pl.when(to != x)
        def _():
            dispatch_copy(m, z, to).wait_send()

    @pl.when(x == 0)
    def _():
        for m in range(MB):
            for j in range(pieces):
                state[m, j * TOK : (j + 1) * TOK] = tokens_ref[m, :, j * PIECE : (j + 1) * PIECE]
            pack_m[0, m] = packing(ids_ref[m : m + 1, :])
            dispatch(0, m, 0)

    for m in range(MB):
        pack_m[1, m] = packing(ids_ref[MB + m : MB + m + 1, :])

    p_row, p_col = iota((128, 128), 0), iota((128, 128), 1)
    perm[...] = ones_where(
        (p_col == ((p_row // 2) % 8) * 16 + (p_row // 16) * 2 + p_row % 2)
        & ((p_row // 2) % 8 < pieces)
    )
    perm_t[...] = ones_where(
        (p_row == ((p_col // 2) % 8) * 16 + (p_col // 16) * 2 + p_col % 2)
        & ((p_col // 2) % 8 < pieces)
    )
    for layer in range(LMAX):
        for m in range(MB):
            ids_col = ids_col_ref[:, layer * MB + m : layer * MB + m + 1]
            hit = ones_where(jnp.broadcast_to(ids_col, (TOK, 128)) == slot_e)
            rank = dot(earlier_t, hit)
            good = (hit > 0) & (rank == (slot_k + 1).astype(jnp.float32))
            for j in range(pieces):
                unpack_m[layer, m, j * TOK : (j + 1) * TOK] = ones_where(good & (slot_j == j))

    @pl.when(x < segments - 1)
    def _():
        ids_copy.wait_recv()
        for m in range(MB):
            pack_m[2, m] = packing(ids_next[m : m + 1, :])

    @pl.when(x > 0)
    def _():
        ids_copy.wait_send()

    for load in loads:
        load.wait()

    def section_of(k):
        total = jnp.int32(0)
        for start in starts[1:]:
            total = total + jnp.where(k >= start, 1, 0)
        return total

    def layer_of(k):
        total = k
        for before, start in zip(starts[:-1], starts[1:]):
            total = total - jnp.where(k >= start, start - before, 0)
        return total

    def state_copy(m):
        return pltpu.make_async_remote_copy(
            src_ref=state.at[m],
            dst_ref=state.at[m],
            send_sem=state_sem.at[0, m],
            recv_sem=state_sem.at[1, m],
            device_id=at(jnp.minimum(x + 1, segments - 1), z, y, c),
            device_id_type=MESH,
        )

    mine = c * Y + y

    def gather_copies(m):
        copies = []
        for d in (2, 1, 3):
            copies.append(
                pltpu.make_async_remote_copy(
                    src_ref=gathered.at[m, mine],
                    dst_ref=gathered.at[m, mine],
                    send_sem=gather_send_sem.at[m, d],
                    recv_sem=gather_sem.at[m, mine],
                    device_id=at(x, z, (y + d) % Y, c),
                    device_id_type=MESH,
                )
            )
        return copies

    def forward(m, yy, i):
        block = c * Y + yy
        return pltpu.make_async_remote_copy(
            src_ref=gathered.at[m, block],
            dst_ref=gathered.at[m, block],
            send_sem=gather_send_sem.at[m, 4 + i],
            recv_sem=gather_sem.at[m, block],
            device_id=at(x, z, y, 1 - c),
            device_id_type=MESH,
        )

    def arrived(m, block):
        pltpu.make_async_copy(
            gathered.at[m, block], gathered.at[m, block], gather_sem.at[m, block]
        ).wait()

    def relay(m, layer):
        for d in range(Z):
            zz = (z + d) % Z
            pltpu.make_async_copy(landed.at[m, zz], landed.at[m, zz], landed_sem.at[m, zz]).wait()
        rows = dot(perm_t[...], landed[m].reshape(128, PIECE))
        square = jnp.zeros((16, 1), jnp.float32)
        for j in range(pieces):
            piece = rows[16 * j : 16 * j + 16]
            square = square + jnp.sum(piece * piece, axis=1, keepdims=True)
        ratio = lax.rsqrt(square / width + 1e-06)
        gain = gain_ref[0, pl.ds(layer, 1), :]
        for j in range(pieces):
            span = slice(j * PIECE, (j + 1) * PIECE)
            gathered[m, mine, :, span] = (
                rows[16 * j : 16 * j + 16] * ratio * gain[:, span]
            ).astype(jnp.bfloat16)
        for copy in gather_copies(m):
            copy.start()
        forward(m, y, 0).start()

    def pass_on(m):
        for i, d in enumerate((1, 3, 2)):
            yy = (y + d) % Y
            arrived(m, c * Y + yy)
            forward(m, yy, i + 1).start()

    def sibling_copy(m):
        return pltpu.make_async_remote_copy(
            src_ref=part.at[m, 1 - c],
            dst_ref=sibling_part.at[m],
            send_sem=sib_sem.at[0, m],
            recv_sem=sib_sem.at[1, m],
            device_id=at(x, z, y, 1 - c),
            device_id_type=MESH,
        )

    def experts(m, layer):
        for yy in range(Y):
            arrived(m, (1 - c) * Y + yy)
        rows = gathered[m].reshape(128, width)
        gate = dot(rows, gate_w[layer])
        up = dot(rows, up_w[layer])
        hidden = (gate * lax.logistic(gate) * up).astype(jnp.bfloat16)
        for j in range(pieces):
            span = slice(j * PIECE, (j + 1) * PIECE)
            part[m, :, :, span] = (
                dot(hidden, down_w[layer, :, span]).astype(jnp.bfloat16).reshape(2, group, PIECE)
            )
        sibling_copy(m).start()

    def reduce_copy(m, d):
        return pltpu.make_async_remote_copy(
            src_ref=pair.at[m, (y + d) % Y],
            dst_ref=reduced.at[m, y],
            send_sem=reduce_send_sem.at[m, d],
            recv_sem=reduce_sem.at[m, y],
            device_id=at(x, z, (y + d) % Y, c),
            device_id_type=MESH,
        )

    def chip_sum(m):
        for copy in gather_copies(m):
            copy.wait_send()
        for i, d in enumerate((0, 1, 3, 2)):
            forward(m, (y + d) % Y, i).wait_send()
        sibling_copy(m).wait_recv()
        for d in (2, 1, 3, 0):
            yy = (y + d) % Y
            start = pl.multiple_of(yy * 16, 16)
            pair[m, yy] = (
                part[m, c, pl.ds(start, 16), :].astype(jnp.float32)
                + sibling_part[m, pl.ds(start, 16), :].astype(jnp.float32)
            ).astype(jnp.bfloat16)
            if d > 0:
                reduce_copy(m, d).start()

    def back_copy(m, zz):
        return pltpu.make_async_remote_copy(
            src_ref=back.at[m, zz],
            dst_ref=returned.at[m, z],
            send_sem=back_sem.at[m, zz],
            recv_sem=returned_sem.at[m, z],
            device_id=at(x, zz, y, c),
            device_id_type=MESH,
        )

    def own_back(m):
        return pltpu.make_async_copy(back.at[m, z], returned.at[m, z], returned_sem.at[m, z])

    def plane_sum(m):
        for d in (1, 3, 2):
            yy = (y + d) % Y
            pltpu.make_async_copy(
                reduced.at[m, yy], reduced.at[m, yy], reduce_sem.at[m, yy]
            ).wait()
        total = []
        for j in range(pieces):
            span = slice(j * PIECE, (j + 1) * PIECE)
            value = pair[m, y, :, span].astype(jnp.float32)
            for d in range(1, Y):
                value = value + reduced[m, (y + d) % Y, :, span].astype(jnp.float32)
            total.append(value.astype(jnp.bfloat16))
        stacked = jnp.concatenate(total, axis=0)
        back[m] = (
            dot(perm[:, : 16 * pieces], stacked).astype(jnp.bfloat16).reshape(Z, 16, PIECE)
        )
        for d in FAR_FIRST[:-1]:
            back_copy(m, (z + d) % Z).start()
        own_back(m).start()

    def combine(m, layer):
        for d in range(Z):
            zz = (z + d) % Z
            pltpu.make_async_copy(
                returned.at[m, zz], returned.at[m, zz], returned_sem.at[m, zz]
            ).wait()
        values = returned[m].reshape(128, PIECE)
        active = layer < depth_ref[0]
        column = jnp.where(layer == 0, scale_ref[:, m : m + 1], scale_ref[:, MB + m : MB + m + 1])
        for j in range(pieces):
            span = slice(j * TOK, (j + 1) * TOK)
            picked = dot(unpack_m[layer, m, span], values)
            before = state[m, span].astype(jnp.float32)
            after = before + column * picked
            state[m, span] = jnp.where(active, after, before).astype(jnp.bfloat16)

    def finish(m):
        sibling_copy(m).wait_send()
        for d in range(1, Y):
            reduce_copy(m, d).wait_send()
        for d in FAR_FIRST[:-1]:
            back_copy(m, (z + d) % Z).wait_send()

    @pl.when(x == 0)
    def _():
        for m in range(MB):
            dispatch_sent(m, 0)

    def step(k, carry):
        section = section_of(k)
        layer = layer_of(k)
        section_after = section_of(k + 1)
        last = section_after != section

        @pl.when(x == section)
        def _():
            relay(0, layer)
            relay(1, layer)
            pass_on(0)
            experts(0, layer)
            pass_on(1)
            chip_sum(0)
            experts(1, layer)
            chip_sum(1)
            plane_sum(0)
            plane_sum(1)
            for m in range(MB):

                @pl.when((layer == 0) & (section > 0))
                def _():
                    pltpu.make_async_copy(state.at[m], state.at[m], state_sem.at[1, m]).wait()

                combine(m, layer)

                @pl.when(k + 1 < steps)
                def _():
                    dispatch(jnp.where(last, 2, 1), m, section_after)

                @pl.when((k + 1 < steps) & last)
                def _():
                    state_copy(m).start()

            for m in range(MB):
                finish(m)

                @pl.when(k + 1 < steps)
                def _():
                    dispatch_sent(m, section_after)

        return carry

    lax.fori_loop(0, steps, step, 0)

    for m in range(MB):
        for j in range(pieces):
            out_ref[0, m, :, j * PIECE : (j + 1) * PIECE] = state[m, j * TOK : (j + 1) * TOK]

    @pl.when(x < segments - 1)
    def _():
        for m in range(MB):
            state_copy(m).wait_send()


def run(depths_static, collective, args):
    tokens, gain, gate, up, down, ids, ids_col, scale, depth = args
    starts, total = [], 0
    for d in depths_static:
        starts.append(total)
        total += d
    width = tokens.shape[2]
    hidden = gate.shape[3]
    lanes = width // PIECE * TOK
    vmem = pl.BlockSpec(memory_space=pltpu.VMEM)
    hbm = pl.BlockSpec(memory_space=pl.ANY)
    bf = jnp.bfloat16
    dma = pltpu.SemaphoreType.DMA
    return pl.pallas_call(
        functools.partial(kernel, tuple(starts), total),
        out_shape=jax.ShapeDtypeStruct((1, MB, TOK, width), bf),
        in_specs=[vmem, vmem, hbm, hbm, hbm, vmem, vmem, vmem, pl.BlockSpec(memory_space=pltpu.SMEM)],
        out_specs=vmem,
        scratch_shapes=[
            pltpu.VMEM((LMAX, width, hidden), bf),
            pltpu.VMEM((LMAX, width, hidden), bf),
            pltpu.VMEM((LMAX, hidden, width), bf),
            pltpu.VMEM((MB, lanes, PIECE), bf),
            pltpu.VMEM((8, lanes), jnp.int32),
            pltpu.VMEM((3, MB, 128, lanes), bf),
            pltpu.VMEM((LMAX, MB, lanes, 128), bf),
            pltpu.VMEM((128, 128), bf),
            pltpu.VMEM((128, 128), bf),
            pltpu.VMEM((MB, Z, 16, PIECE), bf),
            pltpu.VMEM((MB, Z, 16, PIECE), bf),
            pltpu.VMEM((MB, 8, 16, width), bf),
            pltpu.VMEM((MB, 2, Y * 16, width), bf),
            pltpu.VMEM((MB, Y * 16, width), bf),
            pltpu.VMEM((MB, Y, 16, width), bf),
            pltpu.VMEM((MB, Y, 16, width), bf),
            pltpu.VMEM((MB, Z, 16, PIECE), bf),
            pltpu.VMEM((MB, Z, 16, PIECE), bf),
            dma((LMAX, 3)),
            dma((2, MB)),
            dma((2,)),
            dma((MB, Z)),
            dma((MB, Z)),
            dma((MB, 8)),
            dma((MB, 8)),
            dma((2, MB)),
            dma((MB, Y)),
            dma((MB, Y)),
            dma((MB, Z)),
            dma((MB, Z)),
        ],
        compiler_params=pltpu.CompilerParams(
            collective_id=collective, has_side_effects=True, vmem_limit_bytes=48 * 2**20
        ),
        name="relay_layers",
    )(tokens, gain, gate, up, down, ids, ids_col, scale, depth)


def local(tokens, norm_gain, gate_weight, up_weight, down_weight, expert_ids, gate_scale, depths):
    pieces = tokens.shape[2] // PIECE
    ids = expert_ids.reshape(LMAX * MB, TOK)
    ids_rows = jnp.pad(jnp.tile(ids, (1, pieces)), ((0, 8 - LMAX * MB), (0, 0)))
    ids_col = ids.T
    scale = gate_scale.reshape(LMAX * MB, TOK).T
    args = (
        tokens,
        norm_gain,
        gate_weight,
        up_weight,
        down_weight,
        ids_rows,
        ids_col,
        scale,
        depths,
    )
    return run((2, 2, 2, 2), 0, args)


def solution(mesh):
    return jax.shard_map(
        local,
        mesh=mesh,
        in_specs=(
            P(None, "expert", None),
            P("segment", None, None),
            P("segment", None, None, "expert"),
            P("segment", None, None, "expert"),
            P("segment", None, "expert", None),
            P("segment", None, None, "expert"),
            P("segment", None, None, "expert"),
            P("segment"),
        ),
        out_specs=P("segment", None, "expert", None),
        check_vma=False,
    )
```

```python
import functools

import jax
import jax.numpy as jnp
from jax import lax
from jax.experimental import pallas as pl
from jax.experimental.pallas import tpu as pltpu
from jax.sharding import PartitionSpec as P

MESH = pl.DeviceIdType.MESH
LMAX = 2
MB = 2
TOK = 64
Z = 8
Y = 4
PIECE = 512


def iota(shape, dim):
    return lax.broadcasted_iota(jnp.int32, shape, dim)


def ones_where(condition):
    return jnp.where(condition, 1.0, 0.0).astype(jnp.bfloat16)


def dot(a, b):
    return jnp.dot(a, b, preferred_element_type=jnp.float32)


def kernel(
    starts,
    steps,
    tokens_hbm,
    gain_ref,
    gate_hbm,
    up_hbm,
    down_hbm,
    ids_ref,
    scale_ref,
    out_ref,
    gate_w,
    up_w,
    down_w,
    state,
    ids_own,
    ids_next,
    scale_cols,
    mask,
    pack_m,
    unpack_m,
    perm,
    perm_t,
    both,
    sent,
    landed,
    gathered,
    part,
    sibling_part,
    pair,
    reduced,
    back,
    returned,
    token_sem,
    weight_sem,
    state_sem,
    ids_sem,
    sent_sem,
    landed_sem,
    gather_send_sem,
    gather_sem,
    sib_sem,
    reduce_send_sem,
    reduce_sem,
    back_sem,
    returned_sem,
):
    x = lax.axis_index("segment")
    me = lax.axis_index("expert")
    segments = lax.axis_size("segment")
    z = me // (Y * 2)
    y = (me // 2) % Y
    c = me % 2
    width = gathered.shape[3]
    pieces = width // PIECE
    group = Y * 16

    def at(xx, zz, yy, cc):
        return (xx, zz * (Y * 2) + yy * 2 + cc)

    def each(count, body):
        lax.fori_loop(0, count, lambda i, carry: (body(i), carry)[1], 0)

    def far(i):
        return 4 + ((i + 1) // 2) * (1 - 2 * (i % 2))

    def weight_load(layer, i):
        src, dst = ((gate_hbm, gate_w), (up_hbm, up_w), (down_hbm, down_w))[i]
        return pltpu.make_async_copy(src.at[0, layer], dst.at[layer], weight_sem.at[layer, i])

    def token_load(m, j):
        return pltpu.make_async_copy(
            tokens_hbm.at[m, :, pl.ds(j * PIECE, PIECE)],
            state.at[m, pl.ds(j * TOK, TOK)],
            token_sem.at[m, j],
        )

    barrier = pltpu.get_barrier_semaphore()

    def greet(device):
        pl.semaphore_signal(barrier, inc=1, device_id=device, device_id_type=MESH)

    each(Z - 1, lambda i: greet(at(x, (z + i + 1) % Z, y, c)))
    each(Y - 1, lambda i: greet(at(x, z, (y + i + 1) % Y, c)))
    greet(at(x, z, y, 1 - c))

    @pl.when(x > 0)
    def _():
        each(Z, lambda i: greet(at(x - 1, (z + i) % Z, y, c)))

    @pl.when(x < segments - 1)
    def _():
        each(Z, lambda i: greet(at(x + 1, (z + i) % Z, y, c)))

    @pl.when(x == 0)
    def _():
        each(MB * pieces, lambda i: token_load(i // pieces, i % pieces).start())

    for layer in range(LMAX):
        for i in range(3):
            weight_load(layer, i).start()

    lanes = pieces * TOK
    spread = ones_where(iota((TOK, lanes), 0) == iota((TOK, lanes), 1) % TOK)
    row_slot = iota((128, 16), 0)
    to_row = ones_where((row_slot // 16) * 2 + row_slot % 2 == iota((128, 16), 1))
    mask[...] = ones_where((iota((128, lanes), 0) // 2) % 8 == iota((128, lanes), 1) // TOK)
    ids_own[...] = jnp.zeros_like(ids_own)
    ids_own[0 : LMAX * MB, :TOK] = ids_ref[...].astype(jnp.float32)

    def slots(rows_ref, index):
        slot = iota((16, TOK), 0)
        earlier = ones_where(iota((TOK, TOK), 0) <= iota((TOK, TOK), 1))
        ids_row = jnp.broadcast_to(rows_ref[pl.ds(index, 1), :TOK], (16, TOK))
        hit = ones_where(ids_row == (slot // 2).astype(jnp.float32))
        rank = dot(hit, earlier)
        return ones_where((hit > 0) & (rank == (slot % 2 + 1).astype(jnp.float32)))

    def packing(rows_ref, index, which, m):
        wide = dot(slots(rows_ref, index), spread).astype(jnp.bfloat16)
        pack_m[which, m] = dot(to_row, wide).astype(jnp.bfloat16) * mask[...]

    def dispatch_copy(m, zz, to):
        return pltpu.make_async_remote_copy(
            src_ref=sent.at[m, zz],
            dst_ref=landed.at[m, z],
            send_sem=sent_sem.at[m, zz],
            recv_sem=landed_sem.at[m, z],
            device_id=at(to, zz, y, c),
            device_id_type=MESH,
        )

    def own_copy(m):
        return pltpu.make_async_copy(sent.at[m, z], landed.at[m, z], landed_sem.at[m, z])

    def pack(which, m):
        sent[m] = (
            dot(pack_m[which, m], state[m]).astype(jnp.bfloat16).reshape(Z, 16, PIECE)
        )

    def dispatch(m, to):
        each(Z - 1, lambda i: dispatch_copy(m, (z + far(i)) % Z, to).start())

        @pl.when(to == x)
        def _():
            own_copy(m).start()

        @pl.when(to != x)
        def _():
            dispatch_copy(m, z, to).start()

    def dispatch_sent(m, to):
        each(Z - 1, lambda i: dispatch_copy(m, (z + far(i)) % Z, to).wait_send())

        @pl.when(to != x)
        def _():
            dispatch_copy(m, z, to).wait_send()

    @pl.when(x == 0)
    def _():
        each(MB, lambda m: packing(ids_own, m, 0, m))
        each(MB * pieces, lambda i: token_load(i // pieces, i % pieces).wait())
        each(MB, lambda m: pack(0, m))

    @pl.when((x == 0) | (x == segments - 1))
    def _():
        pl.semaphore_wait(barrier, 11 + Z)

    @pl.when((x > 0) & (x < segments - 1))
    def _():
        pl.semaphore_wait(barrier, 11 + 2 * Z)

    @pl.when(x == 0)
    def _():
        each(MB, lambda m: dispatch(m, 0))

    ids_copy = pltpu.make_async_remote_copy(
        src_ref=ids_own,
        dst_ref=ids_next,
        send_sem=ids_sem.at[0],
        recv_sem=ids_sem.at[1],
        device_id=at(jnp.maximum(x - 1, 0), z, y, c),
        device_id_type=MESH,
    )

    @pl.when(x > 0)
    def _():
        ids_copy.start()

    p_row, p_col = iota((128, 128), 0), iota((128, 128), 1)
    perm[...] = ones_where(
        (p_col == ((p_row // 2) % 8) * 16 + (p_row // 16) * 2 + p_row % 2)
        & ((p_row // 2) % 8 < pieces)
    )
    perm_t[...] = ones_where(
        (p_row == ((p_col // 2) % 8) * 16 + (p_col // 16) * 2 + p_col % 2)
        & ((p_col // 2) % 8 < pieces)
    )
    each(MB, lambda m: packing(ids_own, MB + m, 1, m))

    eye = jnp.where(iota((TOK, TOK), 0) == iota((TOK, TOK), 1), 1.0, 0.0)
    transposed = (((1,), (1,)), ((), ()))
    scale_col = lax.dot_general(
        eye,
        scale_ref[...],
        transposed,
        precision=lax.Precision.HIGHEST,
        preferred_element_type=jnp.float32,
    )
    for i in range(LMAX * MB):
        scale_cols[i] = jnp.broadcast_to(scale_col[:, i : i + 1], (TOK, 128))
    from_slot = ones_where((iota((16, 128), 1) // 16) * 2 + iota((16, 128), 1) % 2 == iota((16, 128), 0))
    column_j = (iota((TOK, 128), 1) // 2) % 8

    def unpacking(i):
        turned = lax.dot_general(
            eye.astype(jnp.bfloat16),
            slots(ids_own, i),
            transposed,
            preferred_element_type=jnp.float32,
        )
        wide = dot(turned.astype(jnp.bfloat16), from_slot)
        for j in range(pieces):
            unpack_m[i, j * TOK : (j + 1) * TOK] = jnp.where(column_j == j, wide, 0.0).astype(
                jnp.bfloat16
            )

    each(LMAX * MB, unpacking)

    @pl.when(x < segments - 1)
    def _():
        ids_copy.wait_recv()
        each(MB, lambda m: packing(ids_next, m, 2, m))

    @pl.when(x > 0)
    def _():
        ids_copy.wait_send()

    for layer in range(LMAX):
        for i in range(3):
            weight_load(layer, i).wait()

    def section_of(k):
        total = jnp.int32(0)
        for start in starts[1:]:
            total = total + jnp.where(k >= start, 1, 0)
        return total

    def layer_of(k):
        total = k
        for before, start in zip(starts[:-1], starts[1:]):
            total = total - jnp.where(k >= start, start - before, 0)
        return total

    def state_copy(m):
        return pltpu.make_async_remote_copy(
            src_ref=state.at[m],
            dst_ref=state.at[m],
            send_sem=state_sem.at[0, m],
            recv_sem=state_sem.at[1, m],
            device_id=at(jnp.minimum(x + 1, segments - 1), z, y, c),
            device_id_type=MESH,
        )

    mine = c * Y + y

    def gather_copy(m, d):
        return pltpu.make_async_remote_copy(
            src_ref=gathered.at[m, mine],
            dst_ref=gathered.at[m, mine],
            send_sem=gather_send_sem.at[m, d],
            recv_sem=gather_sem.at[m, mine],
            device_id=at(x, z, (y + d) % Y, c),
            device_id_type=MESH,
        )

    def forward(m, yy):
        block = c * Y + yy
        return pltpu.make_async_remote_copy(
            src_ref=gathered.at[m, block],
            dst_ref=gathered.at[m, block],
            send_sem=gather_send_sem.at[m, 4 + yy],
            recv_sem=gather_sem.at[m, block],
            device_id=at(x, z, y, 1 - c),
            device_id_type=MESH,
        )

    def arrived(m, block):
        pltpu.make_async_copy(
            gathered.at[m, block], gathered.at[m, block], gather_sem.at[m, block]
        ).wait()

    def relay(m, layer):
        each(
            Z,
            lambda zz: pltpu.make_async_copy(
                landed.at[m, zz], landed.at[m, zz], landed_sem.at[m, zz]
            ).wait(),
        )
        rows = dot(perm_t[...], landed[m].reshape(128, PIECE))
        square = jnp.zeros((16, 1), jnp.float32)
        for j in range(pieces):
            piece = rows[16 * j : 16 * j + 16]
            square = square + jnp.sum(piece * piece, axis=1, keepdims=True)
        ratio = lax.rsqrt(square / width + 1e-06)
        gain = gain_ref[0, pl.ds(layer, 1), :]
        for j in range(pieces):
            span = slice(j * PIECE, (j + 1) * PIECE)
            gathered[m, mine, :, span] = (
                rows[16 * j : 16 * j + 16] * ratio * gain[:, span]
            ).astype(jnp.bfloat16)
        each(Y - 1, lambda i: gather_copy(m, (i + 1) % 3 + 1).start())
        forward(m, y).start()

    def pass_on(m):
        def one(i):
            yy = (y + 1 + 2 * i - 3 * (i // 2)) % Y
            arrived(m, c * Y + yy)
            forward(m, yy).start()

        each(Y - 1, one)

    def sibling_copy(m, yy):
        return pltpu.make_async_remote_copy(
            src_ref=part.at[m, 1 - c, yy],
            dst_ref=sibling_part.at[m, yy],
            send_sem=sib_sem.at[0, m, yy],
            recv_sem=sib_sem.at[1, m, yy],
            device_id=at(x, z, y, 1 - c),
            device_id_type=MESH,
        )

    def experts(m, layer):
        each(Y, lambda yy: arrived(m, (1 - c) * Y + yy))

        half = width // 2

        def hidden_part(i):
            span = pl.ds(pl.multiple_of(i * half, 256), half)
            rows = gathered[m, :, :, span].reshape(128, half)
            both[0] += dot(rows, gate_w[layer, span, :])
            both[1] += dot(rows, up_w[layer, span, :])

        both[...] = jnp.zeros_like(both)
        each(2, hidden_part)
        gate, up = both[0], both[1]
        hidden = (gate * lax.logistic(gate) * up).astype(jnp.bfloat16)


        def output_part(i):
            span = pl.ds(pl.multiple_of(i * half, 256), half)
            part[m, :, :, :, span] = (
                dot(hidden, down_w[layer, :, span]).astype(jnp.bfloat16).reshape(2, Y, 16, half)
            )

        each(2, output_part)
        each(Y, lambda i: sibling_copy(m, (y + 2 + i) % Y).start())

    def reduce_copy(m, d):
        return pltpu.make_async_remote_copy(
            src_ref=pair.at[m, (y + d) % Y],
            dst_ref=reduced.at[m, y],
            send_sem=reduce_send_sem.at[m, d],
            recv_sem=reduce_sem.at[m, y],
            device_id=at(x, z, (y + d) % Y, c),
            device_id_type=MESH,
        )

    def chip_sum(m):
        each(Y - 1, lambda i: gather_copy(m, i + 1).wait_send())
        each(Y, lambda i: forward(m, i).wait_send())

        def one(i):
            d = (2 + i) % Y
            yy = (y + d) % Y
            sibling_copy(m, yy).wait_recv()
            pair[m, yy] = (
                part[m, c, yy].astype(jnp.float32) + sibling_part[m, yy].astype(jnp.float32)
            ).astype(jnp.bfloat16)

            @pl.when(d > 0)
            def _():
                reduce_copy(m, d).start()

        each(Y, one)

    def back_copy(m, zz):
        return pltpu.make_async_remote_copy(
            src_ref=back.at[m, zz],
            dst_ref=returned.at[m, z],
            send_sem=back_sem.at[m, zz],
            recv_sem=returned_sem.at[m, z],
            device_id=at(x, zz, y, c),
            device_id_type=MESH,
        )

    def own_back(m):
        return pltpu.make_async_copy(back.at[m, z], returned.at[m, z], returned_sem.at[m, z])

    def plane_sum(m):
        def one(i):
            yy = (y + i + 1) % Y
            pltpu.make_async_copy(
                reduced.at[m, yy], reduced.at[m, yy], reduce_sem.at[m, yy]
            ).wait()

        each(Y - 1, one)
        total = []
        for j in range(pieces):
            span = slice(j * PIECE, (j + 1) * PIECE)
            value = pair[m, y, :, span].astype(jnp.float32)
            for d in range(1, Y):
                value = value + reduced[m, (y + d) % Y, :, span].astype(jnp.float32)
            total.append(value.astype(jnp.bfloat16))
        stacked = jnp.concatenate(total, axis=0)
        back[m] = (
            dot(perm[:, : 16 * pieces], stacked).astype(jnp.bfloat16).reshape(Z, 16, PIECE)
        )
        each(Z - 1, lambda i: back_copy(m, (z + far(i)) % Z).start())
        own_back(m).start()

    def combine(m, layer):
        each(
            Z,
            lambda zz: pltpu.make_async_copy(
                returned.at[m, zz], returned.at[m, zz], returned_sem.at[m, zz]
            ).wait(),
        )
        values = returned[m].reshape(128, PIECE)
        column = scale_cols[layer * MB + m][:, :1]

        def one(j):
            span = pl.ds(pl.multiple_of(j * TOK, TOK), TOK)
            picked = dot(unpack_m[layer * MB + m, span], values)
            before = state[m, span].astype(jnp.float32)
            state[m, span] = (before + column * picked).astype(jnp.bfloat16)

        each(pieces, one)

    def finish(m):
        each(Y, lambda i: sibling_copy(m, i).wait_send())
        each(Y - 1, lambda i: reduce_copy(m, i + 1).wait_send())
        each(Z - 1, lambda i: back_copy(m, (z + far(i)) % Z).wait_send())

    def close(m, k, section, layer):
        after = section_of(k + 1)

        @pl.when((layer == 0) & (section > 0))
        def _():
            pltpu.make_async_copy(state.at[m], state.at[m], state_sem.at[1, m]).wait()

        combine(m, layer)

        @pl.when((layer > 0) | (section == 0))
        def _():
            dispatch_sent(m, x)

        @pl.when(k + 1 < steps)
        def _():
            pack(jnp.where(after != section, 2, 1), m)
            dispatch(m, after)

        @pl.when((k + 1 < steps) & (after != section))
        def _():
            state_copy(m).start()

        finish(m)

    def slot_of_step(u, carry):
        k, u = u // 4, u % 4
        k_late = jnp.where(u == 0, k - 1, k)
        section, layer = section_of(k), layer_of(k)
        section_late, layer_late = section_of(k_late), layer_of(k_late)
        now = (x == section) & (k < steps)
        late = (x == section_late) & (k_late >= 0) & (k_late < steps)
        lagging = jnp.where(u == 0, 1, 0)

        @pl.when(now & ((u == 0) | (u == 2)))
        def _():
            relay(u // 2, layer)

        @pl.when(late & (u < 2))
        def _():
            plane_sum(lagging)

        @pl.when(now & ((u == 0) | (u == 3)))
        def _():
            m = u // 3
            pass_on(m)
            experts(m, layer)
            chip_sum(m)

        @pl.when(late & ((u == 0) | (u == 2)))
        def _():
            close(lagging, k_late, section_late, layer_late)

        return carry

    lax.fori_loop(0, 4 * steps + 1, slot_of_step, 0)

    def write_out(i):
        m, j = i // pieces, i % pieces
        span = pl.ds(pl.multiple_of(j * PIECE, PIECE), PIECE)
        out_ref[0, m, :, span] = state[m, pl.ds(pl.multiple_of(j * TOK, TOK), TOK)]

    each(MB * pieces, write_out)

    @pl.when(x < segments - 1)
    def _():
        for m in range(MB):
            state_copy(m).wait_send()
            dispatch_sent(m, x + 1)


def run(depths_static, collective, args):
    tokens, gain, gate, up, down, ids, scale = args
    starts, total = [], 0
    for d in depths_static:
        starts.append(total)
        total += d
    width = tokens.shape[2]
    hidden = gate.shape[3]
    pieces = width // PIECE
    lanes = pieces * TOK
    vmem = pl.BlockSpec(memory_space=pltpu.VMEM)
    hbm = pl.BlockSpec(memory_space=pl.ANY)
    bf = jnp.bfloat16
    dma = pltpu.SemaphoreType.DMA
    return pl.pallas_call(
        functools.partial(kernel, tuple(starts), total),
        out_shape=jax.ShapeDtypeStruct((1, MB, TOK, width), bf),
        in_specs=[hbm, vmem, hbm, hbm, hbm, vmem, vmem],
        out_specs=vmem,
        scratch_shapes=[
            pltpu.VMEM((LMAX, width, hidden), bf),
            pltpu.VMEM((LMAX, width, hidden), bf),
            pltpu.VMEM((LMAX, hidden, width), bf),
            pltpu.VMEM((MB, lanes, PIECE), bf),
            pltpu.VMEM((8, 128), jnp.float32),
            pltpu.VMEM((8, 128), jnp.float32),
            pltpu.VMEM((LMAX * MB, TOK, 128), jnp.float32),
            pltpu.VMEM((128, lanes), bf),
            pltpu.VMEM((3, MB, 128, lanes), bf),
            pltpu.VMEM((LMAX * MB, lanes, 128), bf),
            pltpu.VMEM((128, 128), bf),
            pltpu.VMEM((128, 128), bf),
            pltpu.VMEM((2, 128, hidden), jnp.float32),
            pltpu.VMEM((MB, Z, 16, PIECE), bf),
            pltpu.VMEM((MB, Z, 16, PIECE), bf),
            pltpu.VMEM((MB, 8, 16, width), bf),
            pltpu.VMEM((MB, 2, Y, 16, width), bf),
            pltpu.VMEM((MB, Y, 16, width), bf),
            pltpu.VMEM((MB, Y, 16, width), bf),
            pltpu.VMEM((MB, Y, 16, width), bf),
            pltpu.VMEM((MB, Z, 16, PIECE), bf),
            pltpu.VMEM((MB, Z, 16, PIECE), bf),
            dma((MB, pieces)),
            dma((LMAX, 3)),
            dma((2, MB)),
            dma((2,)),
            dma((MB, Z)),
            dma((MB, Z)),
            dma((MB, 8)),
            dma((MB, 8)),
            dma((2, MB, Y)),
            dma((MB, Y)),
            dma((MB, Y)),
            dma((MB, Z)),
            dma((MB, Z)),
        ],
        compiler_params=pltpu.CompilerParams(
            collective_id=collective, has_side_effects=True, vmem_limit_bytes=48 * 2**20
        ),
        name="relay_layers",
    )(tokens, gain, gate, up, down, ids, scale)


def depth_kernel(depth_ref, out_ref, mine, send_sem, recv_sem):
    x = lax.axis_index("segment")
    me = lax.axis_index("expert")
    segments = lax.axis_size("segment")
    barrier = pltpu.get_barrier_semaphore()
    for d in range(1, segments):
        pl.semaphore_signal(
            barrier, inc=1, device_id=((x + d) % segments, me), device_id_type=MESH
        )
    mine[...] = jnp.broadcast_to(depth_ref[0], (8, 128))
    out_ref[x] = jnp.broadcast_to(depth_ref[0], (8, 128))
    pl.semaphore_wait(barrier, segments - 1)
    copies = []
    for d in range(1, segments):
        copy = pltpu.make_async_remote_copy(
            src_ref=mine,
            dst_ref=out_ref.at[x],
            send_sem=send_sem.at[d],
            recv_sem=recv_sem.at[x],
            device_id=((x + d) % segments, me),
            device_id_type=MESH,
        )
        copy.start()
        copies.append(copy)
    for d in range(1, segments):
        other = (x + d) % segments
        pltpu.make_async_copy(out_ref.at[other], out_ref.at[other], recv_sem.at[other]).wait()
    for copy in copies:
        copy.wait_send()


def depth_exchange(depths):
    vmem = pl.BlockSpec(memory_space=pltpu.VMEM)
    return pl.pallas_call(
        depth_kernel,
        out_shape=jax.ShapeDtypeStruct((4, 8, 128), jnp.int32),
        in_specs=[pl.BlockSpec(memory_space=pltpu.SMEM)],
        out_specs=vmem,
        scratch_shapes=[
            pltpu.VMEM((8, 128), jnp.int32),
            pltpu.SemaphoreType.DMA((4,)),
            pltpu.SemaphoreType.DMA((4,)),
        ],
        compiler_params=pltpu.CompilerParams(collective_id=0, has_side_effects=True),
        name="share_depths",
    )(depths)


def local(tokens, norm_gain, gate_weight, up_weight, down_weight, expert_ids, gate_scale, depths):
    args = (
        tokens,
        norm_gain,
        gate_weight,
        up_weight,
        down_weight,
        expert_ids.reshape(LMAX * MB, TOK),
        gate_scale.reshape(LMAX * MB, TOK),
    )
    every = depth_exchange(depths)[:, 0, 0]
    code = jnp.sum((every > 1).astype(jnp.int32) * jnp.asarray([1, 2, 4, 8], jnp.int32))
    branches = []
    for number in range(1, 15):
        pattern = tuple(1 + (number >> s) % 2 for s in range(4))
        branches.append(functools.partial(run, pattern, number))
    return lax.switch(code - 1, branches, args)


def solution(mesh):
    return jax.shard_map(
        local,
        mesh=mesh,
        in_specs=(
            P(None, "expert", None),
            P("segment", None, None),
            P("segment", None, None, "expert"),
            P("segment", None, None, "expert"),
            P("segment", None, "expert", None),
            P("segment", None, None, "expert"),
            P("segment", None, None, "expert"),
            P("segment"),
        ),
        out_specs=P("segment", None, "expert", None),
        check_vma=False,
    )
```

```python
import functools

import jax
import jax.numpy as jnp
from jax import lax
from jax.experimental import pallas as pl
from jax.experimental.pallas import tpu as pltpu
from jax.sharding import PartitionSpec as P

MESH = pl.DeviceIdType.MESH
LMAX = 2
MB = 2
TOK = 64
Z = 8
Y = 4
PIECE = 512


def iota(shape, dim):
    return lax.broadcasted_iota(jnp.int32, shape, dim)


def ones_where(condition):
    return jnp.where(condition, 1.0, 0.0).astype(jnp.bfloat16)


def dot(a, b):
    return jnp.dot(a, b, preferred_element_type=jnp.float32)


def kernel(
    starts,
    steps,
    tokens_hbm,
    gain_ref,
    gate_hbm,
    up_hbm,
    down_hbm,
    ids_ref,
    scale_ref,
    depth_ref,
    out_hbm,
    in_w,
    down_w,
    state,
    all_ids,
    scale_cols,
    scale_rows,
    base,
    link,
    link_scale,
    mask,
    pack_m,
    unpack_m,
    perm,
    perm_t,
    both,
    sent,
    landed,
    gathered,
    part,
    sibling_part,
    pair,
    reduced,
    back,
    returned,
    token_sem,
    out_sem,
    weight_sem,
    state_sem,
    ids_sem,
    sent_sem,
    landed_sem,
    gather_send_sem,
    gather_sem,
    sib_sem,
    reduce_send_sem,
    reduce_sem,
    back_sem,
    returned_sem,
):
    x = lax.axis_index("segment")
    me = lax.axis_index("expert")
    segments = lax.axis_size("segment")
    z = me // (Y * 2)
    y = (me // 2) % Y
    c = me % 2
    width = gathered.shape[3]
    pieces = width // PIECE
    group = Y * 16

    def at(xx, zz, yy, cc):
        return (xx, zz * (Y * 2) + yy * 2 + cc)

    def each(count, body):
        lax.fori_loop(0, count, lambda i, carry: (body(i), carry)[1], 0)

    def far(i):
        return 4 + ((i + 1) // 2) * (1 - 2 * (i % 2))

    def chip_order(i):
        return jnp.where(i < 2, 2 + i, 3 - i)

    def weight_load(layer, i):
        src, dst = ((gate_hbm, in_w.at[0]), (up_hbm, in_w.at[1]), (down_hbm, down_w))[i]
        return pltpu.make_async_copy(src.at[0, layer], dst.at[layer], weight_sem.at[layer, i])

    def token_load(m, j):
        return pltpu.make_async_copy(
            tokens_hbm.at[m, :, pl.ds(pl.multiple_of(j * PIECE, PIECE), PIECE)],
            state.at[m, pl.ds(pl.multiple_of(j * TOK, TOK), TOK)],
            token_sem.at[m, j],
        )

    all_ids[...] = jnp.zeros_like(all_ids)
    all_ids[0 : LMAX * MB, :TOK] = ids_ref[...].astype(jnp.float32)
    barrier = pltpu.get_barrier_semaphore()

    def greet(device):
        pl.semaphore_signal(barrier, inc=1, device_id=device, device_id_type=MESH)

    each(Z - 1, lambda i: greet(at(x, (z + i + 1) % Z, y, c)))
    each(Y - 1, lambda i: greet(at(x, z, (y + i + 1) % Y, c)))
    greet(at(x, z, y, 1 - c))

    def greet_beside(i):
        beside = x - 1 + 2 * (i // Z)

        @pl.when((beside >= 0) & (beside < segments))
        def _():
            greet(at(beside, (z + i) % Z, y, c))

    each(2 * Z, greet_beside)

    @pl.when(x == 0)
    def _():
        each(MB * pieces, lambda i: token_load(i // pieces, i % pieces).start())

    for i in range(3):
        each(LMAX, lambda layer: weight_load(layer, i).start())

    lanes = pieces * TOK
    spread = ones_where(iota((TOK, lanes), 0) == iota((TOK, lanes), 1) % TOK)
    row_slot = iota((128, 16), 0)
    to_row = ones_where((row_slot // 16) * 2 + row_slot % 2 == iota((128, 16), 1))
    mask[...] = ones_where((iota((128, lanes), 0) // 2) % 8 == iota((128, lanes), 1) // TOK)

    def slots(index):
        slot = iota((16, TOK), 0)
        earlier = ones_where(iota((TOK, TOK), 0) <= iota((TOK, TOK), 1))
        ids_row = jnp.broadcast_to(all_ids[pl.ds(index, 1), :TOK], (16, TOK))
        hit = ones_where(ids_row == (slot // 2).astype(jnp.float32))
        rank = dot(hit, earlier)
        return ones_where((hit > 0) & (rank == (slot % 2 + 1).astype(jnp.float32)))

    def packing(index, which, m):
        wide = dot(slots(index), spread).astype(jnp.bfloat16)
        pack_m[which, m] = dot(to_row, wide).astype(jnp.bfloat16) * mask[...]

    def dispatch_copy(m, zz, to):
        return pltpu.make_async_remote_copy(
            src_ref=sent.at[m, zz],
            dst_ref=landed.at[m, z],
            send_sem=sent_sem.at[m, zz],
            recv_sem=landed_sem.at[m, z],
            device_id=at(to, zz, y, c),
            device_id_type=MESH,
        )

    def own_copy(m):
        return pltpu.make_async_copy(sent.at[m, z], landed.at[m, z], landed_sem.at[m, z])

    def pack(which, m):
        sent[m] = (
            dot(pack_m[which, m], state[m]).astype(jnp.bfloat16).reshape(Z, 16, PIECE)
        )

    def dispatch(m, to):
        def one(i):
            zz = (z + far(i)) % Z

            @pl.when((zz != z) | (to != x))
            def _():
                dispatch_copy(m, zz, to).start()

        each(Z, one)

        @pl.when(to == x)
        def _():
            own_copy(m).start()

    def dispatch_sent(m, to):
        def one(zz):
            @pl.when((zz != z) | (to != x))
            def _():
                dispatch_copy(m, zz, to).wait_send()

        each(Z, one)

    @pl.when(x == 0)
    def _():
        each(MB, lambda m: packing(m, 0, m))
        each(MB * pieces, lambda i: token_load(i // pieces, i % pieces).wait())
        each(MB, lambda m: pack(0, m))

    @pl.when((x == 0) | (x == segments - 1))
    def _():
        pl.semaphore_wait(barrier, 11 + Z)

    @pl.when((x > 0) & (x < segments - 1))
    def _():
        pl.semaphore_wait(barrier, 11 + 2 * Z)

    @pl.when(x == 0)
    def _():
        each(MB, lambda m: dispatch(m, 0))

    ids_copy = pltpu.make_async_remote_copy(
        src_ref=all_ids.at[0:8],
        dst_ref=all_ids.at[8:16],
        send_sem=ids_sem.at[0],
        recv_sem=ids_sem.at[1],
        device_id=at(jnp.maximum(x - 1, 0), z, y, c),
        device_id_type=MESH,
    )

    @pl.when(x > 0)
    def _():
        ids_copy.start()

    p_row, p_col = iota((128, 128), 0), iota((128, 128), 1)
    perm[...] = ones_where(
        (p_col == ((p_row // 2) % 8) * 16 + (p_row // 16) * 2 + p_row % 2)
        & ((p_row // 2) % 8 < pieces)
    )
    perm_t[...] = ones_where(
        (p_row == ((p_col // 2) % 8) * 16 + (p_col // 16) * 2 + p_col % 2)
        & ((p_col // 2) % 8 < pieces)
    )

    scale = jnp.where(iota((LMAX * MB, TOK), 0) // MB < depth_ref[0], scale_ref[...], 0.0)
    eye = jnp.where(iota((TOK, TOK), 0) == iota((TOK, TOK), 1), 1.0, 0.0)
    transposed = (((1,), (1,)), ((), ()))
    scale_col = lax.dot_general(
        eye,
        scale,
        transposed,
        precision=lax.Precision.HIGHEST,
        preferred_element_type=jnp.float32,
    )
    scale_rows[0 : LMAX * MB] = jnp.dot(
        scale,
        spread.astype(jnp.float32),
        precision=lax.Precision.HIGHEST,
        preferred_element_type=jnp.float32,
    )
    for i in range(LMAX * MB):
        scale_cols[i] = jnp.broadcast_to(scale_col[:, i : i + 1], (TOK, 128))

    from_slot = ones_where((iota((16, 128), 1) // 16) * 2 + iota((16, 128), 1) % 2 == iota((16, 128), 0))
    column_j = (iota((TOK, 128), 1) // 2) % 8

    def unpacking(i):
        turned = lax.dot_general(
            eye.astype(jnp.bfloat16),
            slots(i),
            transposed,
            preferred_element_type=jnp.float32,
        )
        wide = dot(turned.astype(jnp.bfloat16), from_slot)

        def piece(j):
            unpack_m[i, pl.ds(pl.multiple_of(j * TOK, TOK), TOK)] = jnp.where(
                column_j == j, wide, 0.0
            ).astype(jnp.bfloat16)

        each(pieces, piece)

    each(LMAX * MB, unpacking)

    @pl.when(x < segments - 1)
    def _():
        ids_copy.wait_recv()

    def packing_later(i):
        m = i % MB
        packing(jnp.where(i < MB, MB + m, 8 + m), 1 + i // MB, m)

    each(2 * MB, packing_later)

    @pl.when(x > 0)
    def _():
        ids_copy.wait_send()

    for i in range(3):
        each(LMAX, lambda layer: weight_load(layer, i).wait())

    def section_of(k):
        total = jnp.int32(0)
        for start in starts[1:]:
            total = total + jnp.where(k >= start, 1, 0)
        return total

    def layer_of(k):
        total = k
        for before, start in zip(starts[:-1], starts[1:]):
            total = total - jnp.where(k >= start, start - before, 0)
        return total

    def state_copy(m):
        return pltpu.make_async_remote_copy(
            src_ref=state.at[m],
            dst_ref=state.at[m],
            send_sem=state_sem.at[0, m],
            recv_sem=state_sem.at[1, m],
            device_id=at(jnp.minimum(x + 1, segments - 1), z, y, c),
            device_id_type=MESH,
        )

    mine = c * Y + y

    def gather_copy(m, d):
        return pltpu.make_async_remote_copy(
            src_ref=gathered.at[m, mine],
            dst_ref=gathered.at[m, mine],
            send_sem=gather_send_sem.at[m, d],
            recv_sem=gather_sem.at[m, mine],
            device_id=at(x, z, (y + d) % Y, c),
            device_id_type=MESH,
        )

    def forward(m, yy):
        block = c * Y + yy
        return pltpu.make_async_remote_copy(
            src_ref=gathered.at[m, block],
            dst_ref=gathered.at[m, block],
            send_sem=gather_send_sem.at[m, 4 + yy],
            recv_sem=gather_sem.at[m, block],
            device_id=at(x, z, y, 1 - c),
            device_id_type=MESH,
        )

    def arrived(m, block):
        pltpu.make_async_copy(
            gathered.at[m, block], gathered.at[m, block], gather_sem.at[m, block]
        ).wait()

    def relay(m, layer):
        each(
            Z,
            lambda zz: pltpu.make_async_copy(
                landed.at[m, zz], landed.at[m, zz], landed_sem.at[m, zz]
            ).wait(),
        )
        rows = dot(perm_t[...], landed[m].reshape(128, PIECE))
        square = jnp.zeros((16, 1), jnp.float32)
        for j in range(pieces):
            piece = rows[16 * j : 16 * j + 16]
            square = square + jnp.sum(piece * piece, axis=1, keepdims=True)
        ratio = lax.rsqrt(square / width + 1e-06)
        gain = gain_ref[0, pl.ds(layer, 1), :]
        for j in range(pieces):
            span = slice(j * PIECE, (j + 1) * PIECE)
            gathered[m, mine, :, span] = (
                rows[16 * j : 16 * j + 16] * ratio * gain[:, span]
            ).astype(jnp.bfloat16)
        each(Y - 1, lambda i: gather_copy(m, (i + 1) % 3 + 1).start())
        forward(m, y).start()

    def pass_on(m):
        def one(i):
            yy = (y + 1 + 2 * i - 3 * (i // 2)) % Y
            arrived(m, c * Y + yy)
            forward(m, yy).start()

        each(Y - 1, one)

    def sibling_copy(m, yy):
        return pltpu.make_async_remote_copy(
            src_ref=part.at[m, 1 - c, yy],
            dst_ref=sibling_part.at[m, yy],
            send_sem=sib_sem.at[0, m, yy],
            recv_sem=sib_sem.at[1, m, yy],
            device_id=at(x, z, y, 1 - c),
            device_id_type=MESH,
        )

    def experts(m, layer):
        each(Y, lambda yy: arrived(m, (1 - c) * Y + yy))

        half = width // 2

        def hidden_part(i):
            span = pl.ds(pl.multiple_of(i * half, 256), half)
            rows = gathered[m, :, :, span].reshape(128, half)
            both[0] += dot(rows, in_w[0, layer, span, :])
            both[1] += dot(rows, in_w[1, layer, span, :])

        both[...] = jnp.zeros_like(both)
        each(2, hidden_part)
        gate, up = both[0], both[1]
        hidden = (gate * lax.logistic(gate) * up).astype(jnp.bfloat16)


        def output_part(i):
            span = pl.ds(pl.multiple_of(i * half, 256), half)
            part[m, :, :, :, span] = (
                dot(hidden, down_w[layer, :, span]).astype(jnp.bfloat16).reshape(2, Y, 16, half)
            )

        each(2, output_part)
        each(Y, lambda i: sibling_copy(m, (y + chip_order(i)) % Y).start())

    def reduce_copy(m, d):
        return pltpu.make_async_remote_copy(
            src_ref=pair.at[m, (y + d) % Y],
            dst_ref=reduced.at[m, y],
            send_sem=reduce_send_sem.at[m, d],
            recv_sem=reduce_sem.at[m, y],
            device_id=at(x, z, (y + d) % Y, c),
            device_id_type=MESH,
        )

    def chip_sum(m):
        each(Y - 1, lambda i: gather_copy(m, i + 1).wait_send())
        each(Y, lambda i: forward(m, i).wait_send())

        def one(i):
            d = chip_order(i)
            yy = (y + d) % Y
            sibling_copy(m, yy).wait_recv()
            pair[m, yy] = (
                part[m, c, yy].astype(jnp.float32) + sibling_part[m, yy].astype(jnp.float32)
            ).astype(jnp.bfloat16)

            @pl.when(d > 0)
            def _():
                reduce_copy(m, d).start()

        each(Y, one)

    def back_copy(m, zz):
        return pltpu.make_async_remote_copy(
            src_ref=back.at[m, zz],
            dst_ref=returned.at[m, z],
            send_sem=back_sem.at[m, zz],
            recv_sem=returned_sem.at[m, z],
            device_id=at(x, zz, y, c),
            device_id_type=MESH,
        )

    def own_back(m):
        return pltpu.make_async_copy(back.at[m, z], returned.at[m, z], returned_sem.at[m, z])

    def plane_sum(m):
        def one(i):
            yy = (y + i + 1) % Y
            pltpu.make_async_copy(
                reduced.at[m, yy], reduced.at[m, yy], reduce_sem.at[m, yy]
            ).wait()

        each(Y - 1, one)
        total = []
        for j in range(pieces):
            span = slice(j * PIECE, (j + 1) * PIECE)
            value = pair[m, y, :, span].astype(jnp.float32)
            for d in range(1, Y):
                value = value + reduced[m, (y + d) % Y, :, span].astype(jnp.float32)
            total.append(value.astype(jnp.bfloat16))
        stacked = jnp.concatenate(total, axis=0)
        back[m] = (
            dot(perm[:, : 16 * pieces], stacked).astype(jnp.bfloat16).reshape(Z, 16, PIECE)
        )
        each(Z - 1, lambda i: back_copy(m, (z + far(i)) % Z).start())
        own_back(m).start()

    def combine(m, layer):
        values = returned[m].reshape(128, PIECE)
        column = scale_cols[layer * MB + m][:, :1]

        def one(j):
            span = pl.ds(pl.multiple_of(j * TOK, TOK), TOK)
            picked = dot(unpack_m[layer * MB + m, span], values)
            before = state[m, span].astype(jnp.float32)
            state[m, span] = (before + column * picked).astype(jnp.bfloat16)

        each(pieces, one)

    def prepare(m, layer, which):
        rows = pack_m[which, m]
        base[...] = dot(rows, state[m])
        link[...] = dot(rows, unpack_m[layer * MB + m]).astype(jnp.bfloat16)
        scales = jnp.sum(
            rows.astype(jnp.float32) * scale_rows[pl.ds(layer * MB + m, 1), :],
            axis=1,
            keepdims=True,
        )
        link_scale[...] = jnp.broadcast_to(scales, (128, 128))

    def finish(m):
        each(Y, lambda i: sibling_copy(m, i).wait_send())
        each(Y - 1, lambda i: reduce_copy(m, i + 1).wait_send())
        each(Z - 1, lambda i: back_copy(m, (z + far(i)) % Z).wait_send())

    def close(m, k, section, layer):
        after = section_of(k + 1)

        @pl.when((layer == 0) & (section > 0))
        def _():
            pltpu.make_async_copy(state.at[m], state.at[m], state_sem.at[1, m]).wait()

        @pl.when((layer > 0) | (section == 0))
        def _():
            dispatch_sent(m, x)

        @pl.when(k + 1 < steps)
        def _():
            prepare(m, layer, jnp.where(after != section, 2, 1))

        each(
            Z,
            lambda zz: pltpu.make_async_copy(
                returned.at[m, zz], returned.at[m, zz], returned_sem.at[m, zz]
            ).wait(),
        )

        @pl.when(k + 1 < steps)
        def _():
            result = dot(link[...], returned[m].reshape(128, PIECE))
            sent[m] = (
                (base[...] + link_scale[:, :1] * result)
                .astype(jnp.bfloat16)
                .reshape(Z, 16, PIECE)
            )
            dispatch(m, after)

        combine(m, layer)

        @pl.when((k + 1 < steps) & (after != section))
        def _():
            state_copy(m).start()

        finish(m)

    def slot_of_step(u, carry):
        k, u = u // 4, u % 4
        k_late = jnp.where(u == 0, k - 1, k)
        section, layer = section_of(k), layer_of(k)
        section_late, layer_late = section_of(k_late), layer_of(k_late)
        now = (x == section) & (k < steps)
        late = (x == section_late) & (k_late >= 0) & (k_late < steps)
        lagging = jnp.where(u == 0, 1, 0)

        @pl.when(now & ((u == 0) | (u == 2)))
        def _():
            relay(u // 2, layer)

        @pl.when(late & (u < 2))
        def _():
            plane_sum(lagging)

        @pl.when(now & ((u == 0) | (u == 3)))
        def _():
            m = u // 3
            pass_on(m)
            experts(m, layer)
            chip_sum(m)

        @pl.when(late & ((u == 0) | (u == 2)))
        def _():
            close(lagging, k_late, section_late, layer_late)

        return carry

    lax.fori_loop(0, 4 * steps + 1, slot_of_step, 0)

    def write_out(i):
        m, j = i // pieces, i % pieces
        return pltpu.make_async_copy(
            state.at[m, pl.ds(pl.multiple_of(j * TOK, TOK), TOK)],
            out_hbm.at[0, m, :, pl.ds(pl.multiple_of(j * PIECE, PIECE), PIECE)],
            out_sem.at[m, j],
        )

    each(MB * pieces, lambda i: write_out(i).start())
    each(MB * pieces, lambda i: write_out(i).wait())

    def all_sent(m):
        state_copy(m).wait_send()
        dispatch_sent(m, x + 1)

    @pl.when(x < segments - 1)
    def _():
        each(MB, all_sent)


def run(depths_static, collective, args):
    tokens, gain, gate, up, down, ids, scale, depth = args
    starts, total = [], 0
    for d in depths_static:
        starts.append(total)
        total += d
    width = tokens.shape[2]
    hidden = gate.shape[3]
    pieces = width // PIECE
    lanes = pieces * TOK
    vmem = pl.BlockSpec(memory_space=pltpu.VMEM)
    hbm = pl.BlockSpec(memory_space=pl.ANY)
    bf = jnp.bfloat16
    dma = pltpu.SemaphoreType.DMA
    return pl.pallas_call(
        functools.partial(kernel, tuple(starts), total),
        out_shape=jax.ShapeDtypeStruct((1, MB, TOK, width), bf),
        in_specs=[hbm, vmem, hbm, hbm, hbm, vmem, vmem, pl.BlockSpec(memory_space=pltpu.SMEM)],
        out_specs=hbm,
        scratch_shapes=[
            pltpu.VMEM((2, LMAX, width, hidden), bf),
            pltpu.VMEM((LMAX, hidden, width), bf),
            pltpu.VMEM((MB, lanes, PIECE), bf),
            pltpu.VMEM((16, 128), jnp.float32),
            pltpu.VMEM((LMAX * MB, TOK, 128), jnp.float32),
            pltpu.VMEM((8, lanes), jnp.float32),
            pltpu.VMEM((128, PIECE), jnp.float32),
            pltpu.VMEM((128, 128), bf),
            pltpu.VMEM((128, 128), jnp.float32),
            pltpu.VMEM((128, lanes), bf),
            pltpu.VMEM((3, MB, 128, lanes), bf),
            pltpu.VMEM((LMAX * MB, lanes, 128), bf),
            pltpu.VMEM((128, 128), bf),
            pltpu.VMEM((128, 128), bf),
            pltpu.VMEM((2, 128, hidden), jnp.float32),
            pltpu.VMEM((MB, Z, 16, PIECE), bf),
            pltpu.VMEM((MB, Z, 16, PIECE), bf),
            pltpu.VMEM((MB, 8, 16, width), bf),
            pltpu.VMEM((MB, 2, Y, 16, width), bf),
            pltpu.VMEM((MB, Y, 16, width), bf),
            pltpu.VMEM((MB, Y, 16, width), bf),
            pltpu.VMEM((MB, Y, 16, width), bf),
            pltpu.VMEM((MB, Z, 16, PIECE), bf),
            pltpu.VMEM((MB, Z, 16, PIECE), bf),
            dma((MB, pieces)),
            dma((MB, pieces)),
            dma((LMAX, 3)),
            dma((2, MB)),
            dma((2,)),
            dma((MB, Z)),
            dma((MB, Z)),
            dma((MB, 8)),
            dma((MB, 8)),
            dma((2, MB, Y)),
            dma((MB, Y)),
            dma((MB, Y)),
            dma((MB, Z)),
            dma((MB, Z)),
        ],
        compiler_params=pltpu.CompilerParams(
            collective_id=collective, has_side_effects=True, vmem_limit_bytes=48 * 2**20
        ),
        name="relay_layers",
    )(tokens, gain, gate, up, down, ids, scale, depth)


def depth_kernel(depth_ref, code_ref, mine, every, send_sem, recv_sem):
    x = lax.axis_index("segment")
    me = lax.axis_index("expert")
    segments = lax.axis_size("segment")
    barrier = pltpu.get_barrier_semaphore()
    for d in range(1, segments):
        pl.semaphore_signal(
            barrier, inc=1, device_id=((x + d) % segments, me), device_id_type=MESH
        )
    mine[...] = jnp.broadcast_to(depth_ref[0], (8, 128))
    every[x] = jnp.broadcast_to(depth_ref[0], (8, 128))
    pl.semaphore_wait(barrier, segments - 1)
    copies = []
    for d in (2, 1, 3):
        copy = pltpu.make_async_remote_copy(
            src_ref=mine,
            dst_ref=every.at[x],
            send_sem=send_sem.at[d],
            recv_sem=recv_sem.at[x],
            device_id=((x + d) % segments, me),
            device_id_type=MESH,
        )
        copy.start()
        copies.append(copy)
    for d in (1, 3, 2):
        other = (x + d) % segments
        pltpu.make_async_copy(every.at[other], every.at[other], recv_sem.at[other]).wait()
    code = jnp.zeros((8, 128), jnp.int32)
    for s in range(4):
        code = code + jnp.where(every[s] > 1, 1 << s, 0)
    code_ref[0] = jnp.max(jnp.where(code == 1, 9, code)) - 2
    for copy in copies:
        copy.wait_send()


def pattern_of(depths):
    return pl.pallas_call(
        depth_kernel,
        out_shape=jax.ShapeDtypeStruct((1,), jnp.int32),
        in_specs=[pl.BlockSpec(memory_space=pltpu.SMEM)],
        out_specs=pl.BlockSpec(memory_space=pltpu.SMEM),
        scratch_shapes=[
            pltpu.VMEM((8, 128), jnp.int32),
            pltpu.VMEM((4, 8, 128), jnp.int32),
            pltpu.SemaphoreType.DMA((4,)),
            pltpu.SemaphoreType.DMA((4,)),
        ],
        compiler_params=pltpu.CompilerParams(collective_id=0, has_side_effects=True),
        name="share_depths",
    )(depths)[0]


def local(tokens, norm_gain, gate_weight, up_weight, down_weight, expert_ids, gate_scale, depths):
    args = (
        tokens,
        norm_gain,
        gate_weight,
        up_weight,
        down_weight,
        expert_ids.reshape(LMAX * MB, TOK),
        gate_scale.reshape(LMAX * MB, TOK),
        depths,
    )
    branches = []
    for number in range(2, 15):
        pattern = tuple(1 + (number >> s) % 2 for s in range(4))
        branches.append(functools.partial(run, pattern, number))
    return lax.switch(pattern_of(depths), branches, args)


def solution(mesh):
    return jax.shard_map(
        local,
        mesh=mesh,
        in_specs=(
            P(None, "expert", None),
            P("segment", None, None),
            P("segment", None, None, "expert"),
            P("segment", None, None, "expert"),
            P("segment", None, "expert", None),
            P("segment", None, None, "expert"),
            P("segment", None, None, "expert"),
            P("segment"),
        ),
        out_specs=P("segment", None, "expert", None),
        check_vma=False,
    )
```
